32 devices in a mesh: dp: 4 (over x, core), tensor: 8 (over z, y).
Axes of the slice: x: 2, y: 2, z: 4, core: 2. Of those that a mesh axis runs over, the one named last changes fastest.
Arguments:
- inputs: bfloat16 [128, 64, 8192], P('dp', None, 'tensor'), may hold values from -6 to 6
- out_grads: bfloat16 [128, 64, 28672], P('dp', None, 'tensor'), may hold values from -6 to 6
- proj_in: bfloat16 [8192, 64], P('tensor'), may hold values from -0.0625 to 0.0625
- proj_out: bfloat16 [28672, 64], P('tensor'), may hold values from -0.03125 to 0.03125
- counts: int32 [128], P(('dp', 'tensor')), may hold values from 1 to 64, as said below
- starts: int32 [128], P(('dp', 'tensor')), may hold values from 0 to 63, as said below
- queries: bfloat16 [1024, 4096], P('dp'), may hold values from -0.01171875 to 0.01171875
Outputs:
- scores: float32 [128, 1024], P(('dp', 'tensor'))
The draws below stay inside these ranges and needn't reach their ends.
Inputs may be any that keep to these rules, and one draw needn't show every extreme that they name: `counts`: each example holds 1 to 64 tokens; some example holds 64 and some holds 1. starts[e] < counts[e] for every example, so each example has one or more counted positions (weight 1).
All inputs are finite; a program needn't handle non-finite values.
Results may differ from the reference program's by a relative error of at most 0.0029.
Values may be sent and summed in bfloat16 or wider, within the bound.
No kernel may reach another device: no remote copies, remote signals or barrier semaphores. Data moves between devices by JAX's collectives and lax.ppermute only.
A program may use at most 64 MiB of HBM per device.

```python
import jax
import jax.numpy as jnp
from jax import lax

D = 8192
FF = 28672
R = 64
S = 64
QUERIES = 1024
EXAMPLES = 128


def shared_marks(key):
    first_key, second_key = jax.random.split(key)
    position = jnp.arange(EXAMPLES, dtype=jnp.int32)
    counts = jax.random.randint(first_key, (EXAMPLES,), 1, S + 1)
    counts = jnp.where(position == 0, S, counts)
    counts = jnp.where(position == 1, 1, counts)
    counts = jnp.where(position == 2, S, counts)
    starts = jax.random.randint(second_key, (EXAMPLES,), 0, counts)
    starts = jnp.where(position == 0, 0, starts)
    starts = jnp.where(position == 2, S - 1, starts)
    return (counts.astype(jnp.int32), starts.astype(jnp.int32))


def draw_counts(key, part):
    return shared_marks(key)[0]


def draw_starts(key, part):
    return shared_marks(key)[1]


def block_scale(rng, dims, cuts, smallest, largest):
    def one(dim, blocks):
        steps = jax.random.uniform(jax.random.fold_in(jax.random.fold_in(rng, 6), dim), (blocks,), jnp.float32, smallest / len(cuts), largest / len(cuts))
        return jnp.repeat(jnp.exp(steps), dims[dim] // blocks).reshape((-1,) + (1,) * (len(dims) - dim - 1))

    gain = one(*cuts[0])
    for cut in cuts[1:]:
        gain = gain * one(*cut)
    return gain


def bell_draw(rng, shape, spread, bound, cuts=(), kind=jnp.bfloat16):
    array = jax.random.normal(rng, shape, jnp.float32) * spread
    if len(cuts) > 0:
        array = block_scale(rng, shape, cuts, -0.22, 0.18) * array
    return jnp.clip(array, min=-bound, max=bound).astype(kind)


def setup_inputs(seed: int = 0) -> dict:
    seeds = jax.random.split(jax.random.key(seed), 8)
    inputs = bell_draw(seeds[0], (EXAMPLES, S, D), 1.0, 6.0, ((0, 4), (2, 8)))
    out_grads = bell_draw(seeds[1], (EXAMPLES, S, FF), 1.0, 6.0, ((0, 4), (2, 8)))
    proj_in = bell_draw(seeds[2], (D, R), D ** -0.5, 0.0625, ((0, 8),))
    proj_out = bell_draw(seeds[3], (FF, R), FF ** -0.5, 0.03125, ((0, 8),))
    counts = draw_counts(jax.random.fold_in(seeds[7], 71), 0)
    starts = draw_starts(jax.random.fold_in(seeds[7], 71), 0)
    queries = bell_draw(seeds[6], (QUERIES, R * R), (R * R * S) ** -0.5, 0.01171875, ((0, 4),))
    return dict(inputs=inputs, out_grads=out_grads, proj_in=proj_in, proj_out=proj_out, counts=counts, starts=starts, queries=queries)


def reference(inputs, out_grads, proj_in, proj_out, counts, starts, queries):
    total_rows = inputs.shape[0] * inputs.shape[1]
    in_proj = jnp.dot(inputs.reshape(total_rows, -1), proj_in, preferred_element_type=jnp.float32)
    out_proj = jnp.dot(out_grads.reshape(total_rows, -1), proj_out, preferred_element_type=jnp.float32)
    in_proj = in_proj.reshape(inputs.shape[0], inputs.shape[1], -1)
    out_proj = out_proj.reshape(inputs.shape[0], inputs.shape[1], -1)
    position = jnp.arange(inputs.shape[1], dtype=jnp.int32)
    weight = ((position[None, :] >= starts[:, None]) & (position[None, :] < counts[:, None])).astype(jnp.float32)
    out_proj = out_proj * weight[:, :, None]
    grads = jnp.einsum("esi,esj->eij", out_proj, in_proj, precision=lax.Precision.HIGHEST)
    grads = grads.reshape(inputs.shape[0], -1).astype(jnp.bfloat16)
    return lax.dot_general(grads, queries, (((1,), (1,)), ((), ())), preferred_element_type=jnp.float32)
```

```python
import functools
import math

import jax
import jax.numpy as jnp
from jax import lax
from jax.experimental import pallas as pl
from jax.experimental.pallas import tpu as pltpu
from jax.sharding import PartitionSpec as P

DATA_BOUND = 6.0
IN_BOUND = 0.0625
OUT_BOUND = 0.03125
CONTRACT_LAST = (((1,), (1,)), ((), ()))
VMEM_LIMIT = 20 * 1024 * 1024
BLOCK = 1024
FLIGHT = 5


def code_scale(largest):
    return 2.0 ** math.floor(math.log2(65504.0 / (1.01 * largest**0.25)))


def encode(value, scale):
    root = jnp.sqrt(jnp.sqrt(jnp.abs(value))) * scale
    return jnp.where(value < 0, -root, root)


def decode(code, scale):
    code = code * (1.0 / scale)
    square = code * code
    return jnp.where(code < 0, -square * square, square * square)


def project_kernel(offsets, away, first, scale, grads_hbm, inputs_hbm, out_factor, in_factor, *refs):
    refs = list(refs)
    queries_hbm = refs.pop(0) if first else None
    home = len(offsets) - away
    results = [refs.pop(0) for n in (home, away) if n > 0]
    out_held, in_held, queries = (refs.pop(0), refs.pop(0), refs.pop(0)) if first else (out_factor, in_factor, None)
    grads, inputs, sems, extra_sems = refs
    count, chunk, wide = grads.shape
    narrow = inputs.shape[2]
    rank = out_held.shape[0]
    me = lax.axis_index("tensor")
    blocks = [(start, min(BLOCK, wide - start)) for start in range(0, wide, BLOCK)]
    teams = [range(g, min(g + 2, count)) for g in range(0, count, 2)]

    queue = []
    for team in teams:
        for n, (start, width) in enumerate([(0, narrow)] + blocks):
            source, target = (inputs_hbm, inputs) if n == 0 else (grads_hbm, grads)
            queue.append(
                [
                    pltpu.make_async_copy(
                        source.at[pl.ds(pl.multiple_of((me ^ offsets[g]) * chunk, chunk), chunk), pl.ds(start, width)],
                        target.at[g, :, pl.ds(start, width)],
                        sems.at[g, n],
                    )
                    for g in team
                ]
            )
    loads = []
    if first:
        queue.append([pltpu.make_async_copy(queries_hbm, queries, extra_sems.at[2])])
        loads = [
            pltpu.make_async_copy(in_factor, in_held, extra_sems.at[0]),
            pltpu.make_async_copy(out_factor, out_held, extra_sems.at[1]),
        ]
    begun = done = 0

    def begin(upto):
        nonlocal begun
        while begun < min(upto, len(queue)):
            for copy in queue[begun]:
                copy.start()
            begun += 1

    def finish():
        nonlocal done
        for copy in queue[done]:
            copy.wait()
        done += 1
        begin(done + FLIGHT)

    if first:
        loads[0].start()
        begin(1)
        loads[1].start()
    begin(FLIGHT - 1)
    for team in teams:
        span = slice(team[0], team[-1] + 1)
        tokens = len(team) * chunk
        finish()
        if first and team[0] == 0:
            loads[0].wait()
        in_part = lax.dot_general(
            in_held[...], inputs[span].reshape(tokens, narrow), CONTRACT_LAST, preferred_element_type=jnp.float32
        )
        out_part = None
        for n, (start, width) in enumerate(blocks):
            finish()
            if first and team[0] == 0 and n == 0:
                loads[1].wait()
            columns = slice(start, start + width)
            part = lax.dot_general(
                out_held[:, columns],
                grads[span, :, columns].reshape(tokens, width),
                CONTRACT_LAST,
                preferred_element_type=jnp.float32,
            )
            out_part = part if n == 0 else out_part + part
        for n, g in enumerate(team):
            lanes = slice(n * chunk, (n + 1) * chunk)
            for rows, half in ((slice(0, rank), out_part[:, lanes]), (slice(rank, 2 * rank), in_part[:, lanes])):
                if g < home:
                    results[0][g, rows, :] = half
                else:
                    results[-1][g - home, rows, :] = encode(half, scale)
    while done < len(queue):
        finish()


def project(grad_rows, input_rows, factors, offsets, away, queries, chunk, scale):
    first = queries is not None
    wide, narrow = grad_rows.shape[1], input_rows.shape[1]
    rank = factors[0].shape[0]
    count = len(offsets)
    data = grad_rows.dtype
    hbm = pl.BlockSpec(memory_space=pltpu.HBM)
    vmem = pl.BlockSpec(memory_space=pltpu.VMEM)

    def pinned(array):
        return pltpu.with_memory_space_constraint(array, pltpu.HBM)

    operands = [pinned(grad_rows), pinned(input_rows)] + [pinned(f) if first else f for f in factors]
    in_specs = [hbm, hbm] + [hbm if first else vmem] * 2
    shapes = [((n, 2 * rank, chunk), jnp.float32) for n in (count - away, away) if n > 0]
    if first:
        operands.append(pinned(queries))
        in_specs.append(hbm)
        shapes += [((rank, wide), data), ((rank, narrow), data), (queries.shape, data)]
    return pl.pallas_call(
        functools.partial(project_kernel, tuple(offsets), away, first, scale),
        in_specs=in_specs,
        out_specs=[vmem] * len(shapes),
        out_shape=[jax.ShapeDtypeStruct(*shape) for shape in shapes],
        scratch_shapes=[
            pltpu.VMEM((count, chunk, wide), data),
            pltpu.VMEM((count, chunk, narrow), data),
            pltpu.SemaphoreType.DMA((count, -(-wide // BLOCK) + 1)),
            pltpu.SemaphoreType.DMA((3,)),
        ],
        compiler_params=pltpu.CompilerParams(vmem_limit_bytes=VMEM_LIMIT),
        cost_estimate=pl.CostEstimate(
            flops=4 * count * chunk * rank * (wide + narrow),
            bytes_accessed=2 * count * chunk * (wide + narrow),
            transcendentals=0,
        ),
        name="project",
    )(*operands)


def hold_kernel(ours, theirs, held, sems):
    pieces = sems.shape[1]
    size = ours.shape[0]
    rows = size // pieces
    core = lax.axis_index("dp") & 1
    copies = []
    for m, source in enumerate((theirs, ours)):
        start = pl.multiple_of((core ^ (1 - m)) * size, size)
        for n in range(pieces):
            copies.append(
                pltpu.make_async_copy(
                    source.at[pl.ds(n * rows, rows)], held.at[pl.ds(start + n * rows, rows)], sems.at[m, n]
                )
            )
    for copy in copies:
        copy.start()
    for copy in copies:
        copy.wait()


def hold(ours, theirs):
    return pl.pallas_call(
        hold_kernel,
        in_specs=[pl.BlockSpec(memory_space=pl.ANY)] * 2,
        out_specs=pl.BlockSpec(memory_space=pltpu.VMEM),
        out_shape=pltpu.VMEM((2 * ours.shape[0], ours.shape[1]), ours.dtype),
        scratch_shapes=[pltpu.SemaphoreType.DMA((2, 4))],
        compiler_params=pltpu.CompilerParams(vmem_limit_bytes=8 * 1024 * 1024),
        cost_estimate=pl.CostEstimate(flops=0, bytes_accessed=4 * ours.size, transcendentals=0),
        name="hold",
    )(ours, theirs)


def body(inputs, out_grads, proj_in, proj_out, counts, starts, queries):
    local_examples = inputs.shape[0]
    length = inputs.shape[1]
    rank = proj_in.shape[1]
    tensor_size = lax.axis_size("tensor")
    dp_size = lax.axis_size("dp")
    owned = local_examples // tensor_size
    chunk = owned * length
    input_rows = inputs.reshape(local_examples * length, -1)
    grad_rows = out_grads.reshape(local_examples * length, -1)
    largest = DATA_BOUND * max(grad_rows.shape[1] * OUT_BOUND, input_rows.shape[1] * IN_BOUND)
    scale, pair_scale = code_scale(largest), code_scale(2 * largest)

    pairs = tensor_size // 2
    far = list(range(pairs - 1, 0, -1))
    partner = [(i, i ^ 1) for i in range(tensor_size)]

    def received(part, coding):
        return decode(part.astype(jnp.float32), coding)

    coded, out_factor, in_factor, queries = project(
        grad_rows, input_rows, (proj_out.T, proj_in.T), [2 * m + 1 for m in far + [0]], pairs, queries, chunk, scale
    )
    got_far = lax.ppermute(coded[:-1].astype(jnp.float16), "tensor", partner)
    (home,) = project(
        grad_rows, input_rows, (out_factor, in_factor), [2 * m for m in far + [0]], 0, None, chunk, scale
    )
    coded_near = coded[-1] + 0.0 * got_far[0].astype(jnp.float32)
    got_near = lax.ppermute(coded_near.astype(jnp.float16), "tensor", partner)
    leaving = encode(home[:-1] + received(got_far, scale), pair_scale).astype(jnp.float16)
    sent = [
        lax.ppermute(leaving[n], "tensor", [(i, i ^ (2 * m)) for i in range(tensor_size)]) for n, m in enumerate(far)
    ]
    total = home[-1] + received(got_near, scale)
    for part in sent:
        total = total + received(part, pair_scale)

    summed = total.T.reshape(owned, length, 2 * rank)
    position = jnp.arange(length, dtype=jnp.int32)
    weight = (
        (position[None, :] >= starts[:, None]) & (position[None, :] < counts[:, None])
    ).astype(jnp.float32)
    out_proj = summed[:, :, :rank] * weight[:, :, None]
    in_proj = summed[:, :, rank:]
    grads = jnp.einsum("esi,esj->eij", out_proj, in_proj, precision=lax.Precision.HIGH)
    grads = grads.reshape(owned, rank * rank).astype(jnp.bfloat16)

    twin = lax.ppermute(queries, "dp", [(i, i ^ 1) for i in range(dp_size)])
    me = lax.axis_index("dp")
    chips = dp_size // 2
    across = [[(i, i ^ (2 * k + 1)) for i in range(dp_size)] for k in range(chips)]
    rows = jnp.concatenate([grads] + [lax.ppermute(grads, "dp", across[k]) for k in range(1, chips)], axis=0)
    scores = lax.dot_general(rows, hold(queries, twin), CONTRACT_LAST, preferred_element_type=jnp.float32)
    scores = scores.reshape(chips, owned, -1)
    blocks = [scores[0]] + [lax.ppermute(scores[k], "dp", across[k]) for k in range(1, chips)]
    chip = me >> 1
    columns = []
    for c in range(chips):
        column = blocks[0]
        for k in range(1, chips):
            column = jnp.where((chip ^ k) == c, blocks[k], column)
        columns.append(column)
    return jnp.concatenate(columns, axis=1)


def solution(mesh):
    placed = (
        P("dp", None, "tensor"),
        P("dp", None, "tensor"),
        P("tensor", None),
        P("tensor", None),
        P(("dp", "tensor")),
        P(("dp", "tensor")),
        P("dp", None),
    )
    return jax.shard_map(
        body, mesh=mesh, in_specs=placed, out_specs=P(("dp", "tensor"), None), check_vma=False
    )
```

```python
import functools
import math

import jax
import jax.numpy as jnp
from jax import lax
from jax.experimental import pallas as pl
from jax.experimental.pallas import tpu as pltpu
from jax.sharding import PartitionSpec as P

DATA_BOUND = 6.0
IN_BOUND = 0.0625
OUT_BOUND = 0.03125
SMALLEST = 1e-36
CONTRACT_LAST = (((1,), (1,)), ((), ()))
VMEM_LIMIT = 20 * 1024 * 1024
BLOCK = 1280
FLIGHT = 4


def code_scale(largest):
    return 2.0 ** math.floor(math.log2(65504.0 / (1.01 * largest**0.25)))


def encode(value, scale):
    size = jnp.maximum(jnp.abs(value), SMALLEST)
    inverse = lax.rsqrt(size)
    return value * scale * inverse * lax.rsqrt(size * inverse)


def decode(code, scale):
    code = code * (1.0 / scale)
    return (code * jnp.abs(code)) * (code * code)


def project_kernel(offsets, away, first, scale, grads_hbm, inputs_hbm, out_factor, in_factor, *refs):
    refs = list(refs)
    queries_hbm = refs.pop(0) if first else None
    home = len(offsets) - away
    results = [refs.pop(0) for n in (home, away) if n > 0]
    out_held, in_held, queries = (refs.pop(0), refs.pop(0), refs.pop(0)) if first else (out_factor, in_factor, None)
    grads, inputs, sems, extra_sems = refs
    count, chunk, wide = grads.shape
    narrow = inputs.shape[2]
    rank = out_held.shape[0]
    me = lax.axis_index("tensor")
    blocks = [(start, min(BLOCK, wide - start)) for start in range(0, wide, BLOCK)]
    teams = [range(g, min(g + 2, count)) for g in range(0, count, 2)]

    queue = []
    for team in teams:
        for n, (start, width) in enumerate([(0, narrow)] + blocks):
            source, target = (inputs_hbm, inputs) if n == 0 else (grads_hbm, grads)
            queue.append(
                [
                    pltpu.make_async_copy(
                        source.at[pl.ds(pl.multiple_of((me ^ offsets[g]) * chunk, chunk), chunk), pl.ds(start, width)],
                        target.at[g, :, pl.ds(start, width)],
                        sems.at[g, n],
                    )
                    for g in team
                ]
            )
    loads = []
    if first:
        queue.append([pltpu.make_async_copy(queries_hbm, queries, extra_sems.at[2])])
        loads = [
            pltpu.make_async_copy(in_factor, in_held, extra_sems.at[0]),
            pltpu.make_async_copy(out_factor, out_held, extra_sems.at[1]),
        ]
    begun = done = 0

    def begin(upto):
        nonlocal begun
        while begun < min(upto, len(queue)):
            for copy in queue[begun]:
                copy.start()
            begun += 1

    def finish():
        nonlocal done
        for copy in queue[done]:
            copy.wait()
        done += 1
        begin(done + FLIGHT)

    if first:
        loads[0].start()
        begin(1)
        loads[1].start()
    begin(FLIGHT - 1)
    for team in teams:
        span = slice(team[0], team[-1] + 1)
        tokens = len(team) * chunk
        finish()
        if first and team[0] == 0:
            loads[0].wait()
        in_part = lax.dot_general(
            in_held[...], inputs[span].reshape(tokens, narrow), CONTRACT_LAST, preferred_element_type=jnp.float32
        )
        out_part = None
        for n, (start, width) in enumerate(blocks):
            finish()
            if first and team[0] == 0 and n == 0:
                loads[1].wait()
            columns = slice(start, start + width)
            part = lax.dot_general(
                out_held[:, columns],
                grads[span, :, columns].reshape(tokens, width),
                CONTRACT_LAST,
                preferred_element_type=jnp.float32,
            )
            out_part = part if n == 0 else out_part + part
        for n, g in enumerate(team):
            lanes = slice(n * chunk, (n + 1) * chunk)
            for rows, half in ((slice(0, rank), out_part[:, lanes]), (slice(rank, 2 * rank), in_part[:, lanes])):
                if g < home:
                    results[0][g, rows, :] = half
                else:
                    results[-1][g - home, rows, :] = encode(half, scale)
    while done < len(queue):
        finish()


def project(grad_rows, input_rows, factors, offsets, away, queries, chunk, scale):
    first = queries is not None
    wide, narrow = grad_rows.shape[1], input_rows.shape[1]
    rank = factors[0].shape[0]
    count = len(offsets)
    data = grad_rows.dtype
    hbm = pl.BlockSpec(memory_space=pltpu.HBM)
    vmem = pl.BlockSpec(memory_space=pltpu.VMEM)

    def pinned(array):
        return pltpu.with_memory_space_constraint(array, pltpu.HBM)

    operands = [pinned(grad_rows), pinned(input_rows)] + [pinned(f) if first else f for f in factors]
    in_specs = [hbm, hbm] + [hbm if first else vmem] * 2
    shapes = [((n, 2 * rank, chunk), jnp.float32) for n in (count - away, away) if n > 0]
    if first:
        operands.append(pinned(queries))
        in_specs.append(hbm)
        shapes += [((rank, wide), data), ((rank, narrow), data), (queries.shape, data)]
    return pl.pallas_call(
        functools.partial(project_kernel, tuple(offsets), away, first, scale),
        in_specs=in_specs,
        out_specs=[vmem] * len(shapes),
        out_shape=[jax.ShapeDtypeStruct(*shape) for shape in shapes],
        scratch_shapes=[
            pltpu.VMEM((count, chunk, wide), data),
            pltpu.VMEM((count, chunk, narrow), data),
            pltpu.SemaphoreType.DMA((count, -(-wide // BLOCK) + 1)),
            pltpu.SemaphoreType.DMA((3,)),
        ],
        compiler_params=pltpu.CompilerParams(vmem_limit_bytes=VMEM_LIMIT),
        cost_estimate=pl.CostEstimate(
            flops=4 * count * chunk * rank * (wide + narrow),
            bytes_accessed=2 * count * chunk * (wide + narrow),
            transcendentals=0,
        ),
        name="project",
    )(*operands)


def hold_kernel(ours, theirs, held, sems):
    pieces = sems.shape[1]
    size = ours.shape[0]
    rows = size // pieces
    core = lax.axis_index("dp") & 1
    copies = []
    for m, source in enumerate((theirs, ours)):
        start = pl.multiple_of((core ^ (1 - m)) * size, size)
        for n in range(pieces):
            copies.append(
                pltpu.make_async_copy(
                    source.at[pl.ds(n * rows, rows)], held.at[pl.ds(start + n * rows, rows)], sems.at[m, n]
                )
            )
    for copy in copies:
        copy.start()
    for copy in copies:
        copy.wait()


def hold(ours, theirs):
    return pl.pallas_call(
        hold_kernel,
        in_specs=[pl.BlockSpec(memory_space=pl.ANY)] * 2,
        out_specs=pl.BlockSpec(memory_space=pltpu.VMEM),
        out_shape=pltpu.VMEM((2 * ours.shape[0], ours.shape[1]), ours.dtype),
        scratch_shapes=[pltpu.SemaphoreType.DMA((2, 4))],
        compiler_params=pltpu.CompilerParams(vmem_limit_bytes=8 * 1024 * 1024),
        cost_estimate=pl.CostEstimate(flops=0, bytes_accessed=4 * ours.size, transcendentals=0),
        name="hold",
    )(ours, theirs)


def body(inputs, out_grads, proj_in, proj_out, counts, starts, queries):
    local_examples = inputs.shape[0]
    length = inputs.shape[1]
    rank = proj_in.shape[1]
    tensor_size = lax.axis_size("tensor")
    dp_size = lax.axis_size("dp")
    owned = local_examples // tensor_size
    chunk = owned * length
    input_rows = inputs.reshape(local_examples * length, -1)
    grad_rows = out_grads.reshape(local_examples * length, -1)
    largest = DATA_BOUND * max(grad_rows.shape[1] * OUT_BOUND, input_rows.shape[1] * IN_BOUND)
    scale, pair_scale = code_scale(largest), code_scale(2 * largest)

    pairs = tensor_size // 2
    far = list(range(pairs - 1, 0, -1))
    partner = [(i, i ^ 1) for i in range(tensor_size)]

    def received(part, coding):
        return decode(part.astype(jnp.float32), coding)

    coded, out_factor, in_factor, queries = project(
        grad_rows, input_rows, (proj_out.T, proj_in.T), [2 * m + 1 for m in far + [0]], pairs, queries, chunk, scale
    )
    got_far = lax.ppermute(coded[:-1].astype(jnp.float16), "tensor", partner)
    (home,) = project(
        grad_rows, input_rows, (out_factor, in_factor), [2 * m for m in far + [0]], 0, None, chunk, scale
    )
    coded_near = coded[-1] + 0.0 * got_far[0].astype(jnp.float32)
    got_near = lax.ppermute(coded_near.astype(jnp.float16), "tensor", partner)
    leaving = encode(home[:-1] + received(got_far, scale), pair_scale).astype(jnp.float16)
    sent = [
        lax.ppermute(leaving[n], "tensor", [(i, i ^ (2 * m)) for i in range(tensor_size)]) for n, m in enumerate(far)
    ]
    total = home[-1] + received(got_near, scale)
    for part in sent:
        total = total + received(part, pair_scale)

    summed = total.T.reshape(owned, length, 2 * rank)
    position = jnp.arange(length, dtype=jnp.int32)
    weight = (
        (position[None, :] >= starts[:, None]) & (position[None, :] < counts[:, None])
    ).astype(jnp.float32)
    out_proj = summed[:, :, :rank] * weight[:, :, None]
    in_proj = summed[:, :, rank:]
    grads = jnp.einsum("esi,esj->eij", out_proj, in_proj, precision=lax.Precision.HIGH)
    grads = grads.reshape(owned, rank * rank).astype(jnp.bfloat16)

    twin = lax.ppermute(queries, "dp", [(i, i ^ 1) for i in range(dp_size)])
    me = lax.axis_index("dp")
    chips = dp_size // 2
    across = [[(i, i ^ (2 * k + 1)) for i in range(dp_size)] for k in range(chips)]
    rows = jnp.concatenate([grads] + [lax.ppermute(grads, "dp", across[k]) for k in range(1, chips)], axis=0)
    scores = lax.dot_general(rows, hold(queries, twin), CONTRACT_LAST, preferred_element_type=jnp.float32)
    scores = scores.reshape(chips, owned, -1)
    blocks = [scores[0]] + [lax.ppermute(scores[k], "dp", across[k]) for k in range(1, chips)]
    chip = me >> 1
    columns = []
    for c in range(chips):
        column = blocks[0]
        for k in range(1, chips):
            column = jnp.where((chip ^ k) == c, blocks[k], column)
        columns.append(column)
    return jnp.concatenate(columns, axis=1)


def solution(mesh):
    placed = (
        P("dp", None, "tensor"),
        P("dp", None, "tensor"),
        P("tensor", None),
        P("tensor", None),
        P(("dp", "tensor")),
        P(("dp", "tensor")),
        P("dp", None),
    )
    return jax.shard_map(
        body, mesh=mesh, in_specs=placed, out_specs=P(("dp", "tensor"), None), check_vma=False
    )
```
